32 devices in a mesh: pipe: 4 (over y, core), expert: 8 (over z, x).
Axes of the slice: x: 2, y: 2, z: 4, core: 2. Of those that a mesh axis runs over, the one named last changes fastest.
Arguments:
- grad_in: bfloat16 [4, 512, 2048], P('pipe', 'expert'), may hold values from -6 to 6
- head_grad: bfloat16 [512, 2048], P('expert'), may hold values from -6 to 6
- router_logits: float32 [4, 2, 512, 8], P('pipe', None, 'expert'), may hold values from -8 to 304
- route_ids: int32 [4, 2, 512, 2], P('pipe', None, 'expert'), may hold values from 0 to 7, all different within a row; in each aligned block of 64 rows (0 to 63, 64 to 127, ..., all dimensions but the last counted through in order) at most 24 rows name the same one
- gate_act: bfloat16 [4, 2, 6144, 192], P('pipe', None, 'expert'), may hold values from -6 to 6
- up_act: bfloat16 [4, 2, 6144, 192], P('pipe', None, 'expert'), may hold values from -6 to 6
- router_weight: bfloat16 [4, 2048, 8], P('pipe'), may hold values from -0.125 to 0.125
- gate_weight: bfloat16 [4, 6144, 2048], P('pipe', 'expert'), may hold values from -0.125 to 0.125
- up_weight: bfloat16 [4, 6144, 2048], P('pipe', 'expert'), may hold values from -0.125 to 0.125
- down_weight: bfloat16 [4, 6144, 2048], P('pipe', 'expert'), may hold values from -0.21875 to 0.21875
- z_weight: float32 [], replicated, may hold values from 0.5 to 2
Outputs:
- grad_out: bfloat16 [4, 512, 2048], P('pipe', 'expert')
- down_grad: bfloat16 [4, 6144, 2048], P('pipe', 'expert')
The draws below stay inside these ranges and needn't reach their ends.
Inputs may be any that keep to these rules, and one draw needn't show every extreme that they name: `route_ids`: each row names 2 different experts. Within the 64 tokens of one index of expert, for one section and micro-batch, no expert is named more than 24 times, a bound that some block reaches.
All inputs are finite; a program needn't handle non-finite values.
Results may differ from the reference program's by a relative error of at most 0.0068.
Values may be sent and summed in bfloat16 or wider, within the bound.
A program may use at most 64 MiB of HBM per device.

```python
import math
from functools import partial
import jax
import jax.numpy as jnp
import numpy as np
from jax import lax

D = 2048
HID = 768
EXPERTS = 8
TOP = 2
MICRO = 2
TOK = 64
CAP = 24
SECTIONS = 4
TOKENS = 512
SLOTS = 192
N_EXPERT = 8


def draw_router_logits(key, part):
    shape = (SECTIONS, MICRO, TOKENS, EXPERTS)
    first_key = jax.random.fold_in(key, 0)
    return jnp.clip(2.0 * jax.random.normal(first_key, shape, jnp.float32), -8.0, 8.0)


def level_of(own_key, dims, cuts, least, largest):
    level = 1.0
    for dim, shards_of in cuts:
        draws = jax.random.uniform(jax.random.fold_in(jax.random.fold_in(own_key, 6), dim), (shards_of,), jnp.float32, least / len(cuts), largest / len(cuts))
        level = level * jnp.repeat(jnp.exp(draws), dims[dim] // shards_of).reshape((-1,) + (1,) * (len(dims) - 1 - dim))
    return level


def deal_out(stream_key, own, number, rows, amount, top, bound, lean):
    order = jax.random.permutation(stream_key, amount)
    heavy_load, common = shares(amount, rows * top, bound, lean, True), shares(amount, rows * top, bound, lean, False)
    places = jnp.arange(amount)

    def named(lengths, turn):
        used = int((lengths > 0).sum())
        fixed = max(1, used // 4)
        moved = fixed + (places - fixed + turn * (used - fixed)) % max(1, amount - fixed)
        return jnp.zeros((amount,), jnp.int32).at[order[jnp.where(places < fixed, places, moved)]].set(jnp.asarray(lengths, jnp.int32))

    lengths = jnp.where(number % 4 == 0, named(heavy_load, number // 4), named(common, number - number // 4 - 1))
    mixed = jax.random.permutation(jax.random.fold_in(own, 3), amount)
    source_of, receiver = mixed[0:amount // 2 * 2:2], mixed[1:amount // 2 * 2:2]
    room = jnp.minimum(lengths[source_of] - 1, bound - lengths[receiver]) // 2
    room = jnp.where((source_of == order[0]) | (receiver == order[0]) | (lengths[receiver] == 0), 0, jnp.maximum(room, 0))
    moved = jax.random.randint(jax.random.fold_in(own, 4), (amount // 2,), 0, 1 << 20) % (room + 1)
    lengths = lengths.at[source_of].add(-moved).at[receiver].add(moved)
    members = jnp.searchsorted(jnp.cumsum(lengths), jnp.arange(rows * top), side="right").astype(jnp.int32)
    grid = members.reshape(top, rows).T
    grid = grid[jax.random.permutation(jax.random.fold_in(own, 1), rows)]
    turn = jax.random.randint(jax.random.fold_in(own, 2), (rows, 1), 0, top)
    return jnp.take_along_axis(grid, (jnp.arange(top)[None, :] + turn) % top, axis=1)


def shares(number_of, total, bound, skew, full):
    loads = [(1 << 20) // math.isqrt(rank ** skew) + 1 for rank in range(1, number_of + 1)]
    largest = bound if full else min(bound, max(-(-total // number_of), total * loads[0] // sum(loads)))
    least = 1 if total - largest >= number_of - 1 else 0
    counts, surplus = [largest] + [least] * (number_of - 1), total - largest - least * (number_of - 1)
    while surplus > 0:
        candidates = [i for i in range(1, number_of) if counts[i] < largest] or [i for i in range(1, number_of) if counts[i] < bound]
        whole, remaining = sum([loads[i] for i in candidates]), surplus
        for i in candidates:
            more = min(bound - counts[i], max(1, remaining * loads[i] // whole), surplus)
            counts[i] = counts[i] + more
            surplus = surplus - more
    return np.array(counts)


def centred(rng, dims, width, limit, cuts=(), kind=jnp.bfloat16):
    values = width * jax.random.normal(rng, dims, jnp.float32)
    if cuts:
        values = values * level_of(rng, dims, cuts, -0.22, 0.18)
    return jnp.clip(values, -limit, limit).astype(kind)


def setup_inputs(seed: int = 0) -> dict:
    seeds = jax.random.split(jax.random.key(seed), 12)
    grad_in = centred(seeds[0], (SECTIONS, TOKENS, D), 1.0, 6.0, ((0, 4), (1, 8)))
    head_grad = centred(seeds[1], (TOKENS, D), 1.0, 6.0, ((0, 8),))
    router_logits = draw_router_logits(jax.random.fold_in(seeds[11], 71), 0)
    route_ids_keys = jax.random.split(jax.random.fold_in(seeds[3], 1), SECTIONS * MICRO * TOKENS // TOK)
    route_ids_turns = jax.random.permutation(jax.random.fold_in(seeds[3], 3), SECTIONS * MICRO * TOKENS // TOK)
    route_ids = jax.vmap(lambda own, number: deal_out(jax.random.fold_in(seeds[3], 2), own, number, TOK, EXPERTS, TOP, CAP, 2))(route_ids_keys, route_ids_turns).reshape((SECTIONS, MICRO, TOKENS, TOP))
    gate_act = centred(seeds[4], (SECTIONS, MICRO, EXPERTS * HID, SLOTS), 1.0, 6.0, ((0, 4), (2, 8)))
    up_act = centred(seeds[5], (SECTIONS, MICRO, EXPERTS * HID, SLOTS), 1.0, 6.0, ((0, 4), (2, 8)))
    router_weight = centred(seeds[6], (SECTIONS, D, EXPERTS), D ** -0.5, 0.125, ((0, 4),))
    gate_weight = centred(seeds[7], (SECTIONS, EXPERTS * HID, D), D ** -0.5, 0.125, ((0, 4), (1, 8)))
    up_weight = centred(seeds[8], (SECTIONS, EXPERTS * HID, D), D ** -0.5, 0.125, ((0, 4), (1, 8)))
    down_weight = centred(seeds[9], (SECTIONS, EXPERTS * HID, D), HID ** -0.5, 0.21875, ((0, 4), (1, 8)))
    z_weight = jnp.clip(jnp.exp(jax.random.uniform(seeds[10], (), jnp.float32, math.log(0.5), math.log(2.0))), 0.5, 2.0)
    return {"grad_in": grad_in, "head_grad": head_grad, "router_logits": router_logits, "route_ids": route_ids, "gate_act": gate_act, "up_act": up_act, "router_weight": router_weight, "gate_weight": gate_weight, "up_weight": up_weight, "down_weight": down_weight, "z_weight": z_weight}


def slot_index(id_block, experts, capacity):
    flat_ids = id_block.reshape(-1)
    onehot = (flat_ids[:, None] == jnp.arange(experts, dtype=jnp.int32)[None, :]).astype(jnp.int32)
    earlier = jnp.cumsum(onehot, axis=0) - onehot
    within = lax.optimization_barrier(jnp.sum(earlier * onehot, axis=1))
    return (flat_ids * capacity + within).reshape(id_block.shape).astype(jnp.int32)

def route_gates(logits, id_rows):
    chosen = jnp.take_along_axis(logits, id_rows, axis=1)
    row_top = lax.optimization_barrier(jnp.max(chosen, axis=1, keepdims=True))
    weights = jnp.exp(chosen - row_top)
    return weights / lax.optimization_barrier(jnp.sum(weights, axis=1, keepdims=True))

def logit_grad(logits, id_rows, gate_vals, prob_grad, z_weight):
    mean_grad = lax.optimization_barrier(jnp.sum(gate_vals * prob_grad, axis=1, keepdims=True))
    chosen = gate_vals * (prob_grad - mean_grad)
    onehot = (id_rows[:, :, None] == jnp.arange(logits.shape[1], dtype=jnp.int32)[None, None, :]).astype(jnp.float32)
    routed = lax.optimization_barrier(jnp.sum(onehot * chosen[:, :, None], axis=1))
    row_top = lax.optimization_barrier(jnp.max(logits, axis=1, keepdims=True))
    shifted = jnp.exp(logits - row_top)
    denom_sum = lax.optimization_barrier(jnp.sum(shifted, axis=1, keepdims=True))
    log_total = row_top + jnp.log(denom_sum)
    return routed + z_weight * 2.0 * log_total * (shifted / denom_sum)

def expert_pass(inputs):
    slot_rows, slot_gate, gate_pre, up_pre, w_gate, w_up, w_down = inputs
    slices = N_EXPERT // EXPERTS
    raw_grad = jnp.dot(slot_rows, w_down.T, preferred_element_type=jnp.float32)
    gate_f = gate_pre.astype(jnp.float32)
    up_f = up_pre.astype(jnp.float32)
    logistic = jax.nn.sigmoid(gate_f)
    swish = gate_f * logistic
    hidden = swish * up_f
    row_count = raw_grad.shape[0]
    piece_len = raw_grad.shape[1] // slices
    prob_part = lax.optimization_barrier(jnp.sum((hidden * raw_grad).reshape(row_count, slices, piece_len), axis=2)).astype(jnp.bfloat16)
    prob_part = lax.optimization_barrier(prob_part)
    prob_grad = lax.optimization_barrier(jnp.sum(prob_part.astype(jnp.float32), axis=1))
    gate_col = slot_gate.astype(jnp.float32)[:, None]
    hid_grad = gate_col * raw_grad
    gate_grad = (hid_grad * up_f * logistic * (1.0 + gate_f * (1.0 - logistic))).astype(jnp.bfloat16)
    up_grad = (hid_grad * swish).astype(jnp.bfloat16)
    gate_blocks = gate_grad.astype(jnp.float32).reshape(row_count, slices, piece_len)
    up_blocks = up_grad.astype(jnp.float32).reshape(row_count, slices, piece_len)
    wg_blocks = w_gate.astype(jnp.float32).reshape(w_gate.shape[0], slices, piece_len)
    wu_blocks = w_up.astype(jnp.float32).reshape(w_up.shape[0], slices, piece_len)
    partial_sum = jnp.einsum('rsw,dsw->srd', gate_blocks, wg_blocks, precision=lax.Precision.HIGHEST)
    partial_sum = partial_sum + jnp.einsum('rsw,dsw->srd', up_blocks, wu_blocks, precision=lax.Precision.HIGHEST)
    rounded = lax.optimization_barrier(partial_sum.astype(jnp.bfloat16))
    slot_grad = lax.optimization_barrier(jnp.sum(rounded.astype(jnp.float32), axis=0))
    scaled = (hidden * gate_col).astype(jnp.bfloat16)
    weight_grad = jnp.dot(scaled.T, slot_rows, preferred_element_type=jnp.float32)
    return (slot_grad, prob_grad, weight_grad)

def section_pass(incoming, logits, id_rows, gate_pre, up_pre, w_router, w_gate, w_up, w_down, z_weight):
    blocks = id_rows.reshape(N_EXPERT, TOK, TOP)
    slot_ids = jax.vmap(partial(slot_index, experts=EXPERTS, capacity=CAP))(blocks)
    gate_vals = route_gates(logits, id_rows)
    sent_gates = gate_vals.astype(jnp.bfloat16)
    source = jnp.arange(N_EXPERT, dtype=jnp.int32)[:, None, None] * jnp.ones_like(slot_ids)
    values = jnp.broadcast_to(incoming.reshape(N_EXPERT, TOK, 1, D), (N_EXPERT, TOK, TOP, D))
    buffer = jnp.zeros((N_EXPERT, EXPERTS * CAP, D), jnp.bfloat16).at[source, slot_ids].set(values)
    gate_buffer = jnp.zeros((N_EXPERT, EXPERTS * CAP), jnp.bfloat16).at[source, slot_ids].set(sent_gates.reshape(N_EXPERT, TOK, TOP))
    slot_rows = buffer.reshape(N_EXPERT, EXPERTS, CAP, D).transpose(1, 0, 2, 3).reshape(EXPERTS, SLOTS, D)
    slot_gate = gate_buffer.reshape(N_EXPERT, EXPERTS, CAP).transpose(1, 0, 2).reshape(EXPERTS, SLOTS)
    gate_slots = gate_pre.reshape(EXPERTS, HID, SLOTS).transpose(0, 2, 1)
    up_slots = up_pre.reshape(EXPERTS, HID, SLOTS).transpose(0, 2, 1)
    wg_all = w_gate.reshape(EXPERTS, HID, D).transpose(0, 2, 1)
    wu_all = w_up.reshape(EXPERTS, HID, D).transpose(0, 2, 1)
    wd_all = w_down.reshape(EXPERTS, HID, D)
    slot_grad, prob_grad, weight_grad = lax.map(expert_pass, (slot_rows, slot_gate, gate_slots, up_slots, wg_all, wu_all, wd_all))
    returned = slot_grad.reshape(EXPERTS, N_EXPERT, CAP, D).transpose(1, 0, 2, 3).reshape(N_EXPERT, EXPERTS * CAP, D)
    returned_prob = prob_grad.reshape(EXPERTS, N_EXPERT, CAP).transpose(1, 0, 2).reshape(N_EXPERT, EXPERTS * CAP)
    expert_grad = lax.optimization_barrier(jnp.sum(returned[source, slot_ids], axis=2)).reshape(TOKENS, D)
    token_prob = returned_prob[source, slot_ids].reshape(TOKENS, TOP)
    logit_part = logit_grad(logits, id_rows, gate_vals, token_prob, z_weight).astype(jnp.bfloat16)
    router_part = jnp.dot(logit_part, w_router.T, preferred_element_type=jnp.float32)
    input_grad = (incoming.astype(jnp.float32) + expert_grad + router_part).astype(jnp.bfloat16)
    return (input_grad, weight_grad.reshape(EXPERTS * HID, D))

def reference(grad_in, head_grad, router_logits, route_ids, gate_act, up_act, router_weight, gate_weight, up_weight, down_weight, z_weight):

    def first_pass(section_idx):
        return section_pass(grad_in[section_idx], router_logits[section_idx, 0], route_ids[section_idx, 0], gate_act[section_idx, 0], up_act[section_idx, 0], router_weight[section_idx], gate_weight[section_idx], up_weight[section_idx], down_weight[section_idx], z_weight)
    passed, weight_first = lax.map(first_pass, jnp.arange(SECTIONS, dtype=jnp.int32))
    incoming_all = jnp.concatenate([passed[1:], head_grad[None]], axis=0)

    def second_pass(section_idx):
        input_grad, weight_grad = section_pass(incoming_all[section_idx], router_logits[section_idx, 1], route_ids[section_idx, 1], gate_act[section_idx, 1], up_act[section_idx, 1], router_weight[section_idx], gate_weight[section_idx], up_weight[section_idx], down_weight[section_idx], z_weight)
        return (input_grad, (weight_grad + weight_first[section_idx]).astype(jnp.bfloat16))
    grad_out, down_grad = lax.map(second_pass, jnp.arange(SECTIONS, dtype=jnp.int32))
    return (grad_out, down_grad)
```

```python
import functools

import jax
import jax.numpy as jnp
from jax import lax
from jax.experimental import pallas as pl
from jax.experimental.pallas import tpu as pltpu
from jax.sharding import PartitionSpec as P

EXPERTS = 8
CAP = 24
TOP = 2
F32 = jnp.float32
BF16 = jnp.bfloat16
D0, R0, D1, R1 = 0, 1, 2, 3


def iota_f(shape, dim):
    return lax.broadcasted_iota(jnp.int32, shape, dim).astype(F32)


def dot(a, b):
    return jnp.dot(a, b, preferred_element_type=F32)


def kernel(
    n, pipes,
    grad_ref, head_ref, logits_ref, ids_ref, zw_ref, wr_ref, ga_hbm, ua_hbm, wg_hbm, wu_hbm, wd_hbm,
    out_ref, dg_hbm,
    sbuf, rbuf, gsend, grecv, psend, precv, hsend, hrecv, g1_ref,
    x_ref, scaled_ref, ggt_ref, ugt_ref, dgv, ga_ref, ua_ref, wg_ref, wu_ref, wd_ref,
    ssem, rsem, gssem, grsem, pssem, prsem, hsem, lsem,
):
    me = lax.axis_index("expert")
    pipe = lax.axis_index("pipe")
    down = lax.rem(pipe + pipes - 1, pipes)
    up = lax.rem(pipe + 1, pipes)
    slices = n // EXPERTS
    tok, dim = grad_ref.shape
    hid = wd_ref.shape[0]
    width = n * CAP
    cols = 512 if dim % 512 == 0 else dim
    ht = 256 if hid % 256 == 0 else hid

    loads = [
        pltpu.make_async_copy(src, dst, lsem.at[i])
        for i, (src, dst) in enumerate(
            [(wd_hbm, wd_ref), (ga_hbm, ga_ref), (ua_hbm, ua_ref), (wg_hbm, wg_ref), (wu_hbm, wu_ref)]
        )
    ]
    for load in loads:
        load.start()

    barrier = pltpu.get_barrier_semaphore()

    def greet(p, carry):
        pl.semaphore_signal(
            barrier, inc=1, device_id=(pipe, lax.rem(me + p, n)), device_id_type=pl.DeviceIdType.MESH
        )
        return carry

    lax.fori_loop(1, n, greet, 0)
    for other in (down, up):
        pl.semaphore_signal(barrier, inc=1, device_id=(other, me), device_id_type=pl.DeviceIdType.MESH)

    def peer_copy(src, dst, s, r, p):
        return pltpu.make_async_remote_copy(
            src_ref=src, dst_ref=dst, send_sem=s, recv_sem=r,
            device_id=(pipe, p), device_id_type=pl.DeviceIdType.MESH,
        )

    def each_peer(body):
        def step(p, carry):
            body(lax.rem(me + p, n))
            return carry

        lax.fori_loop(1, n, step, 0)

    def tiles(total, size, body):
        def step(i, carry):
            body(pl.ds(pl.multiple_of(i * size, size), size))
            return carry

        lax.fori_loop(0, total // size, step, 0)

    def route(m):
        z = logits_ref[m]
        ids = ids_ref[m].astype(F32)
        ecol = iota_f((tok, EXPERTS), 1)
        picks = [ids[:, k : k + 1] for k in range(TOP)]
        named = [jnp.where(i == ecol, 1.0, 0.0) for i in picks]
        lower = jnp.where(iota_f((tok, tok), 0) > iota_f((tok, tok), 1), 1.0, 0.0).astype(BF16)
        earlier = dot(lower, (named[0] + named[1]).astype(BF16))
        ranks = [jnp.sum(a * earlier, axis=1, keepdims=True) for a in named]
        chosen = [jnp.sum(a * z, axis=1, keepdims=True) for a in named]
        top = jnp.maximum(chosen[0], chosen[1])
        w = [jnp.exp(c - top) for c in chosen]
        gates = [v / (w[0] + w[1]) for v in w]
        q = iota_f((tok, EXPERTS * CAP), 1)
        spread = sum(jnp.where(i * CAP + r == q, 1.0, 0.0) for i, r in zip(picks, ranks))
        if slices == 1:
            gather = spread.astype(BF16)
        else:
            q = iota_f((tok, width), 1)
            member = jnp.floor((q + 0.5) / CAP)
            place = jnp.floor((member + 0.5) / slices) * CAP + (q - member * CAP)
            gather = sum(jnp.where(i * CAP + r == place, 1.0, 0.0) for i, r in zip(picks, ranks)).astype(BF16)
        owner = jnp.floor((iota_f((tok, n), 1) + 0.5) / slices)
        owned = [jnp.where(i == owner, 1.0, 0.0) for i in picks]
        lane = iota_f((tok, width), 1)
        base = (me * CAP).astype(F32)
        at = [jnp.where(r + base == lane, 1.0, 0.0) for r in ranks]
        gate_rows = sum(
            dot((o * g.astype(BF16).astype(F32)).T.astype(BF16), a.astype(BF16))
            for o, g, a in zip(owned, gates, at)
        )
        z_top = jnp.max(z, axis=1, keepdims=True)
        shifted = jnp.exp(z - z_top)
        denom = jnp.sum(shifted, axis=1, keepdims=True)
        z_term = zw_ref[0, 0] * 2.0 * (z_top + jnp.log(denom)) * (shifted / denom)
        return dict(
            named=named, gates=gates, spread_t=spread.T.astype(BF16), gather=gather, owned=owned, at=at,
            gate_rows=gate_rows, z_term=z_term,
        )

    def send_rows(phase, by_expert):
        def go(d):
            src = sbuf.at[phase, d // slices if by_expert else d]
            peer_copy(src, rbuf.at[phase, me], ssem.at[phase, d], rsem.at[phase, me], d).start()

        each_peer(go)

    def wait_rows(phase):
        def go(d):
            peer_copy(rbuf.at[phase, d], rbuf.at[phase, d], ssem.at[phase, d], rsem.at[phase, d], d).wait_recv()

        each_peer(go)

    def dispatch(phase, spread_t, src):
        def body(c):
            rows = dot(spread_t, src[:, c])
            for e in range(EXPERTS):
                sbuf[phase, e, :, c] = rows[e * CAP : (e + 1) * CAP].astype(BF16)

        tiles(dim, cols, body)
        send_rows(phase, True)
        rbuf[phase, me] = sbuf[phase, me // slices]

    def joined(phase, c):
        return jnp.concatenate([rbuf[phase, j, :, c].astype(F32) for j in range(n)], axis=0).astype(BF16)

    def local(m, phase, gate_row):
        def fill(c):
            x_ref[m, :, c] = joined(phase, c)

        tiles(dim, cols, fill)
        prob = jnp.zeros((1, width), F32)
        for h in range(0, hid, ht):
            rows = pl.ds(h, ht)
            raw = lax.dot_general(
                wd_ref[rows, :], x_ref[m], (((1,), (1,)), ((), ())), preferred_element_type=F32
            )
            g = ga_ref[m, rows, :].astype(F32)
            u = ua_ref[m, rows, :].astype(F32)
            logistic = jax.nn.sigmoid(g)
            swish = g * logistic
            hidden = swish * u
            prob = prob + jnp.sum(hidden * raw, axis=0, keepdims=True)
            hid_grad = gate_row * raw
            gate_grad = hid_grad * u * logistic * (1.0 + g * (1.0 - logistic))
            up_grad = hid_grad * swish
            scaled_ref[m, rows, :] = (hidden * gate_row).astype(BF16)
            ggt_ref[:, rows] = gate_grad.T.astype(BF16)
            ugt_ref[:, rows] = up_grad.T.astype(BF16)
        psend[m] = jnp.broadcast_to(prob, (16, width)).astype(BF16)

    def give_back(m, phase):
        def go(d):
            peer_copy(psend.at[m], precv.at[m, me], pssem.at[m, d], prsem.at[m, me], d).start()

        each_peer(go)

        def body(c):
            part = dot(ggt_ref[...], wg_ref[:, c]) + dot(ugt_ref[...], wu_ref[:, c])
            for j in range(n):
                sbuf[phase, j, :, c] = part[j * CAP : (j + 1) * CAP].astype(BF16)

        tiles(dim, cols, body)
        send_rows(phase, False)
        rbuf[phase, me] = sbuf[phase, me]
        precv[m, me] = psend[m]

    def combine(m, phase, info, src, dst):
        def arrived(d):
            peer_copy(psend.at[m], precv.at[m, d], pssem.at[m, d], prsem.at[m, d], d).wait_recv()

        each_peer(arrived)
        probs = [jnp.zeros((tok, width), F32) for _ in range(TOP)]
        for d in range(n):
            row = precv[m, d].astype(F32)[0:1]
            probs = [p + o[:, d : d + 1] * row for p, o in zip(probs, info["owned"])]
        probs = [jnp.sum(p * a, axis=1, keepdims=True) for p, a in zip(probs, info["at"])]
        gates = info["gates"]
        mean = gates[0] * probs[0] + gates[1] * probs[1]
        logit = info["z_term"]
        for k in range(TOP):
            logit = logit + info["named"][k] * (gates[k] * (probs[k] - mean))
        logit = logit.astype(BF16)
        wait_rows(phase)

        def body(c):
            total = src[:, c].astype(F32) + dot(info["gather"], joined(phase, c))
            dst[:, c] = (total + dot(logit, wr_ref[:, c])).astype(BF16)

        tiles(dim, cols, body)

    first = route(0)
    pl.semaphore_wait(barrier, n + 1)
    dispatch(D0, first["spread_t"], grad_ref)
    second = route(1)
    half = lax.broadcasted_iota(jnp.int32, (16, width), 0) < 8
    for d in range(n):
        gsend[d] = jnp.where(half, first["gate_rows"][d : d + 1], second["gate_rows"][d : d + 1]).astype(BF16)

    def go_gates(d):
        peer_copy(gsend.at[d], grecv.at[me], gssem.at[d], grsem.at[me], d).start()

    each_peer(go_gates)
    grecv[me] = gsend[me]

    def come_gates(d):
        peer_copy(gsend.at[d], grecv.at[d], gssem.at[d], grsem.at[d], d).wait_recv()

    each_peer(come_gates)
    gate_all = jnp.zeros((16, width), F32)
    for j in range(n):
        gate_all = gate_all + grecv[j].astype(F32)

    for load in loads:
        load.wait()
    wait_rows(D0)
    local(0, D0, gate_all[0:1])
    give_back(0, R0)
    combine(0, R0, first, grad_ref, hsend)
    pass_on = pltpu.make_async_remote_copy(
        src_ref=hsend, dst_ref=hrecv, send_sem=hsem.at[0], recv_sem=hsem.at[1],
        device_id=(down, me), device_id_type=pl.DeviceIdType.MESH,
    )
    pass_on.start()
    pass_on.wait_recv()
    is_last = pipe == pipes - 1
    g1_ref[...] = jnp.where(is_last, head_ref[...], hrecv[...])
    dispatch(D1, second["spread_t"], g1_ref)
    wait_rows(D1)
    local(1, D1, gate_all[8:9])
    give_back(1, R1)

    def weigh(c):
        total = dot(scaled_ref[0], x_ref[0, :, c]) + dot(scaled_ref[1], x_ref[1, :, c])
        dgv[:, c] = total.astype(BF16)

    tiles(dim, 256 if dim % 256 == 0 else dim, weigh)
    store = pltpu.make_async_copy(dgv, dg_hbm, lsem.at[0])
    store.start()
    combine(1, R1, second, g1_ref, out_ref)
    store.wait()
    pass_on.wait_send()

    def drain(d):
        for phase in range(4):
            src = sbuf.at[phase, d]
            peer_copy(src, src, ssem.at[phase, d], rsem.at[phase, d], d).wait_send()
        for m in range(2):
            peer_copy(psend.at[m], precv.at[m, d], pssem.at[m, d], prsem.at[m, d], d).wait_send()
        peer_copy(gsend.at[d], grecv.at[d], gssem.at[d], grsem.at[d], d).wait_send()

    each_peer(drain)


def per_device(
    grad_in, head_grad, router_logits, route_ids, gate_act, up_act, router_weight,
    gate_weight, up_weight, down_weight, z_weight,
):
    n = lax.axis_size("expert")
    pipes = lax.axis_size("pipe")
    tok, dim = head_grad.shape
    hid = down_weight.shape[1]
    width = n * CAP
    vmem = pl.BlockSpec(memory_space=pltpu.VMEM)
    smem = pl.BlockSpec(memory_space=pltpu.SMEM)
    hbm = pl.BlockSpec(memory_space=pl.ANY)
    dma = pltpu.SemaphoreType.DMA
    out, dg = pl.pallas_call(
        functools.partial(kernel, n, pipes),
        out_shape=(
            jax.ShapeDtypeStruct((tok, dim), BF16),
            jax.ShapeDtypeStruct((hid, dim), BF16),
        ),
        in_specs=[vmem, vmem, vmem, vmem, smem, vmem, hbm, hbm, hbm, hbm, hbm],
        out_specs=(vmem, hbm),
        scratch_shapes=[
            pltpu.VMEM((4, n, CAP, dim), BF16),
            pltpu.VMEM((4, n, CAP, dim), BF16),
            pltpu.VMEM((n, 16, width), BF16),
            pltpu.VMEM((n, 16, width), BF16),
            pltpu.VMEM((2, 16, width), BF16),
            pltpu.VMEM((2, n, 16, width), BF16),
            pltpu.VMEM((tok, dim), BF16),
            pltpu.VMEM((tok, dim), BF16),
            pltpu.VMEM((tok, dim), BF16),
            pltpu.VMEM((2, width, dim), BF16),
            pltpu.VMEM((2, hid, width), BF16),
            pltpu.VMEM((width, hid), BF16),
            pltpu.VMEM((width, hid), BF16),
            pltpu.VMEM((hid, dim), BF16),
            pltpu.VMEM((2, hid, width), BF16),
            pltpu.VMEM((2, hid, width), BF16),
            pltpu.VMEM((hid, dim), BF16),
            pltpu.VMEM((hid, dim), BF16),
            pltpu.VMEM((hid, dim), BF16),
            dma((4, n)), dma((4, n)), dma((n,)), dma((n,)), dma((2, n)), dma((2, n)), dma((2,)), dma((5,)),
        ],
        compiler_params=pltpu.CompilerParams(
            collective_id=0, has_side_effects=True, vmem_limit_bytes=56 * 1024 * 1024
        ),
        cost_estimate=pl.CostEstimate(
            flops=16 * hid * width * dim, bytes_accessed=8 * hid * dim, transcendentals=2 * hid * width
        ),
    )(
        grad_in[0], head_grad, router_logits[0], route_ids[0], z_weight.reshape(1, 1),
        router_weight[0].T, gate_act[0], up_act[0], gate_weight[0], up_weight[0], down_weight[0],
    )
    return out[None], dg[None]


def solution(mesh):
    return jax.shard_map(
        per_device,
        mesh=mesh,
        in_specs=(
            P("pipe", "expert", None),
            P("expert", None),
            P("pipe", None, "expert", None),
            P("pipe", None, "expert", None),
            P("pipe", None, "expert", None),
            P("pipe", None, "expert", None),
            P("pipe", None, None),
            P("pipe", "expert", None),
            P("pipe", "expert", None),
            P("pipe", "expert", None),
            P(),
        ),
        out_specs=(P("pipe", "expert", None), P("pipe", "expert", None)),
        check_vma=False,
    )
```

```python
import functools

import jax
import jax.numpy as jnp
from jax import lax
from jax.experimental import pallas as pl
from jax.experimental.pallas import tpu as pltpu
from jax.sharding import PartitionSpec as P

EXPERTS = 8
CAP = 24
TOP = 2
F32 = jnp.float32
BF16 = jnp.bfloat16
D0, R0, D1, R1 = 0, 1, 2, 3
HALVES = 2


def iota_f(shape, dim):
    return lax.broadcasted_iota(jnp.int32, shape, dim).astype(F32)


def dot(a, b):
    return jnp.dot(a, b, preferred_element_type=F32)


def kernel(
    n, pipes,
    grad_ref, head_ref, logits_ref, ids_ref, zw_ref, wr_ref, ga_hbm, ua_hbm, wg_hbm, wu_hbm, wd_hbm,
    out_ref, dg_hbm,
    sbuf, rbuf, gsend, grecv, psend, precv, hsend, hrecv, g1_ref,
    x_ref, scaled_ref, st_ref, ggt_ref, ugt_ref, dgv, ga_ref, ua_ref, wg_ref, wu_ref, wd_ref,
    ssem, rsem, gssem, grsem, pssem, prsem, hsem, lsem,
):
    me = lax.axis_index("expert")
    pipe = lax.axis_index("pipe")
    down = lax.rem(pipe + pipes - 1, pipes)
    up = lax.rem(pipe + 1, pipes)
    slices = n // EXPERTS
    tok, dim = grad_ref.shape
    hid = wd_ref.shape[0]
    width = n * CAP
    part = dim // HALVES
    cols = 512 if part % 512 == 0 else part
    ht = 256 if hid % 256 == 0 else hid

    loads = [
        pltpu.make_async_copy(src, dst, lsem.at[i])
        for i, (src, dst) in enumerate(
            [(wd_hbm, wd_ref), (ga_hbm, ga_ref), (ua_hbm, ua_ref), (wg_hbm, wg_ref), (wu_hbm, wu_ref)]
        )
    ]
    for load in loads:
        load.start()

    barrier = pltpu.get_barrier_semaphore()

    def greet(p, carry):
        pl.semaphore_signal(
            barrier, inc=1, device_id=(pipe, lax.rem(me + p, n)), device_id_type=pl.DeviceIdType.MESH
        )
        return carry

    lax.fori_loop(1, n, greet, 0)
    for other in (down, up):
        pl.semaphore_signal(barrier, inc=1, device_id=(other, me), device_id_type=pl.DeviceIdType.MESH)

    def peer_copy(src, dst, s, r, p):
        return pltpu.make_async_remote_copy(
            src_ref=src, dst_ref=dst, send_sem=s, recv_sem=r,
            device_id=(pipe, p), device_id_type=pl.DeviceIdType.MESH,
        )

    def each_peer(body):
        def step(p, carry):
            body(lax.rem(me + p, n))
            return carry

        lax.fori_loop(1, n, step, 0)

    def tiles(total, size, body):
        def step(i, carry):
            body(pl.ds(pl.multiple_of(i * size, size), size))
            return carry

        lax.fori_loop(0, total // size, step, 0)

    def route(m):
        z = logits_ref[m].T
        ids = ids_ref[m].astype(F32)
        ecol = iota_f((tok, EXPERTS), 1)
        picks = [jnp.broadcast_to(ids[k : k + 1], (EXPERTS, tok)).T[:, 0:1] for k in range(TOP)]
        named = [jnp.where(i == ecol, 1.0, 0.0) for i in picks]
        lower = jnp.where(iota_f((tok, tok), 0) > iota_f((tok, tok), 1), 1.0, 0.0).astype(BF16)
        earlier = dot(lower, (named[0] + named[1]).astype(BF16))
        ranks = [jnp.sum(a * earlier, axis=1, keepdims=True) for a in named]
        chosen = [jnp.sum(a * z, axis=1, keepdims=True) for a in named]
        top = jnp.maximum(chosen[0], chosen[1])
        w = [jnp.exp(c - top) for c in chosen]
        gates = [v / (w[0] + w[1]) for v in w]
        q = iota_f((tok, EXPERTS * CAP), 1)
        spread = sum(jnp.where(i * CAP + r == q, 1.0, 0.0) for i, r in zip(picks, ranks))
        if slices == 1:
            gather = spread.astype(BF16)
        else:
            q = iota_f((tok, width), 1)
            member = jnp.floor((q + 0.5) / CAP)
            place = jnp.floor((member + 0.5) / slices) * CAP + (q - member * CAP)
            gather = sum(jnp.where(i * CAP + r == place, 1.0, 0.0) for i, r in zip(picks, ranks)).astype(BF16)
        owner = jnp.floor((iota_f((tok, n), 1) + 0.5) / slices)
        owned = [jnp.where(i == owner, 1.0, 0.0) for i in picks]
        lane = iota_f((tok, width), 1)
        base = (me * CAP).astype(F32)
        at = [jnp.where(r + base == lane, 1.0, 0.0) for r in ranks]
        gate_rows = sum(
            dot((o * g.astype(BF16).astype(F32)).T.astype(BF16), a.astype(BF16))
            for o, g, a in zip(owned, gates, at)
        )
        z_top = jnp.max(z, axis=1, keepdims=True)
        shifted = jnp.exp(z - z_top)
        denom = jnp.sum(shifted, axis=1, keepdims=True)
        z_term = zw_ref[0, 0] * 2.0 * (z_top + jnp.log(denom)) * (shifted / denom)
        return dict(
            named=named, gates=gates, spread_t=spread.T.astype(BF16), gather=gather, owned=owned, at=at,
            gate_rows=gate_rows, z_term=z_term,
        )

    def send_rows(phase, h, by_expert):
        def go(d):
            src = sbuf.at[phase, h, d // slices if by_expert else d]
            peer_copy(src, rbuf.at[phase, h, me], ssem.at[phase, h, d], rsem.at[phase, h, me], d).start()

        each_peer(go)

    def wait_rows(phase, h):
        def go(d):
            ref = rbuf.at[phase, h, d]
            peer_copy(ref, ref, ssem.at[phase, h, d], rsem.at[phase, h, d], d).wait_recv()

        each_peer(go)

    def half_tiles(body):
        for i in range(part // cols):
            body(slice(i * cols, (i + 1) * cols))

    def dispatch(phase, h, spread_t, src):
        def body(c):
            rows = dot(spread_t, src[:, h * part + c.start : h * part + c.stop])
            for e in range(EXPERTS):
                sbuf[phase, h, e, :, c] = rows[e * CAP : (e + 1) * CAP].astype(BF16)

        half_tiles(body)
        send_rows(phase, h, True)
        rbuf[phase, h, me] = sbuf[phase, h, me // slices]

    def joined(phase, h, c):
        return jnp.concatenate([rbuf[phase, h, j, :, c].astype(F32) for j in range(n)], axis=0).astype(BF16)

    def local(m, phase, gate_col):
        for h in range(HALVES):
            wait_rows(phase, h)

            def fill(c):
                x_ref[m, :, h * part + c.start : h * part + c.stop] = joined(phase, h, c)

            half_tiles(fill)
        prob = jnp.zeros((width, 1), F32)
        for h in range(0, hid, ht):
            rows = slice(h, h + ht)
            raw = lax.dot_general(
                x_ref[m], wd_ref[rows, :], (((1,), (1,)), ((), ())), preferred_element_type=F32
            )
            g = ga_ref[m, :, rows].astype(F32)
            u = ua_ref[m, :, rows].astype(F32)
            logistic = jax.nn.sigmoid(g)
            swish = g * logistic
            hidden = swish * u
            prob = prob + jnp.sum(hidden * raw, axis=1, keepdims=True)
            hid_grad = gate_col * raw
            gate_grad = hid_grad * u * logistic * (1.0 + g * (1.0 - logistic))
            scaled_ref[m, :, rows] = (hidden * gate_col).astype(BF16)
            ggt_ref[:, rows] = gate_grad.astype(BF16)
            ugt_ref[:, rows] = (hid_grad * swish).astype(BF16)
        psend[m] = jnp.broadcast_to(prob, (width, 128)).T[0:16].astype(BF16)

    def give_back(m, phase):
        def go(d):
            peer_copy(psend.at[m], precv.at[m, me], pssem.at[m, d], prsem.at[m, me], d).start()

        each_peer(go)
        for h in range(HALVES):

            def body(c):
                w = slice(h * part + c.start, h * part + c.stop)
                total = dot(ggt_ref[...], wg_ref[:, w]) + dot(ugt_ref[...], wu_ref[:, w])
                for j in range(n):
                    sbuf[phase, h, j, :, c] = total[j * CAP : (j + 1) * CAP].astype(BF16)

            half_tiles(body)
            send_rows(phase, h, False)
            rbuf[phase, h, me] = sbuf[phase, h, me]
        precv[m, me] = psend[m]

    def logits_back(m, info):
        def arrived(d):
            peer_copy(psend.at[m], precv.at[m, d], pssem.at[m, d], prsem.at[m, d], d).wait_recv()

        each_peer(arrived)
        probs = [jnp.zeros((tok, width), F32) for _ in range(TOP)]
        for d in range(n):
            row = precv[m, d].astype(F32)[0:1]
            probs = [p + o[:, d : d + 1] * row for p, o in zip(probs, info["owned"])]
        probs = [jnp.sum(p * a, axis=1, keepdims=True) for p, a in zip(probs, info["at"])]
        gates = info["gates"]
        mean = gates[0] * probs[0] + gates[1] * probs[1]
        logit = info["z_term"]
        for k in range(TOP):
            logit = logit + info["named"][k] * (gates[k] * (probs[k] - mean))
        return logit.astype(BF16)

    def combine(phase, h, info, logit, src, store_to):
        wait_rows(phase, h)

        def body(c):
            w = slice(h * part + c.start, h * part + c.stop)
            total = src[:, w].astype(F32) + dot(info["gather"], joined(phase, h, c))
            store_to(h, c, w, (total + dot(logit, wr_ref[:, w])).astype(BF16))

        half_tiles(body)

    first = route(0)
    pl.semaphore_wait(barrier, n + 1)
    for h in range(HALVES):
        dispatch(D0, h, first["spread_t"], grad_ref)
    second = route(1)
    half = lax.broadcasted_iota(jnp.int32, (16, width), 0) < 8
    for d in range(n):
        gsend[d] = jnp.where(half, first["gate_rows"][d : d + 1], second["gate_rows"][d : d + 1]).astype(BF16)

    def go_gates(d):
        peer_copy(gsend.at[d], grecv.at[me], gssem.at[d], grsem.at[me], d).start()

    each_peer(go_gates)
    grecv[me] = gsend[me]

    def come_gates(d):
        peer_copy(gsend.at[d], grecv.at[d], gssem.at[d], grsem.at[d], d).wait_recv()

    each_peer(come_gates)
    gate_all = jnp.zeros((16, width), F32)
    for j in range(n):
        gate_all = gate_all + grecv[j].astype(F32)

    for load in loads:
        load.wait()
    gate_cols = gate_all.T
    local(0, D0, gate_cols[:, 0:1])
    give_back(0, R0)
    logit = logits_back(0, first)

    def keep(h, c, w, value):
        hsend[h, :, c] = value

    def pass_on(h):
        return pltpu.make_async_remote_copy(
            src_ref=hsend.at[h], dst_ref=hrecv.at[h], send_sem=hsem.at[0, h], recv_sem=hsem.at[1, h],
            device_id=(down, me), device_id_type=pl.DeviceIdType.MESH,
        )

    is_last = pipe == pipes - 1
    for h in range(HALVES):
        combine(R0, h, first, logit, grad_ref, keep)
        pass_on(h).start()
    for h in range(HALVES):
        pass_on(h).wait_recv()
        w = slice(h * part, (h + 1) * part)
        g1_ref[:, w] = jnp.where(is_last, head_ref[:, w], hrecv[h])
        dispatch(D1, h, second["spread_t"], g1_ref)
    local(1, D1, gate_cols[:, 8:9])
    give_back(1, R1)

    for m in range(2):
        st_ref[m] = scaled_ref[m].astype(F32).T.astype(BF16)

    def weigh(c):
        total = dot(st_ref[0], x_ref[0, :, c]) + dot(st_ref[1], x_ref[1, :, c])
        dgv[:, c] = total.astype(BF16)

    tiles(dim, 256 if dim % 256 == 0 else dim, weigh)
    store = pltpu.make_async_copy(dgv, dg_hbm, lsem.at[0])
    store.start()
    logit = logits_back(1, second)

    def write(h, c, w, value):
        out_ref[:, w] = value

    for h in range(HALVES):
        combine(R1, h, second, logit, g1_ref, write)
    store.wait()
    for h in range(HALVES):
        pass_on(h).wait_send()

    def drain(d):
        for phase in range(4):
            for h in range(HALVES):
                src = sbuf.at[phase, h, d]
                peer_copy(src, src, ssem.at[phase, h, d], rsem.at[phase, h, d], d).wait_send()
        for m in range(2):
            peer_copy(psend.at[m], precv.at[m, d], pssem.at[m, d], prsem.at[m, d], d).wait_send()
        peer_copy(gsend.at[d], grecv.at[d], gssem.at[d], grsem.at[d], d).wait_send()

    each_peer(drain)


def per_device(
    grad_in, head_grad, router_logits, route_ids, gate_act, up_act, router_weight,
    gate_weight, up_weight, down_weight, z_weight,
):
    n = lax.axis_size("expert")
    pipes = lax.axis_size("pipe")
    tok, dim = head_grad.shape
    hid = down_weight.shape[1]
    width = n * CAP
    vmem = pl.BlockSpec(memory_space=pltpu.VMEM)
    smem = pl.BlockSpec(memory_space=pltpu.SMEM)
    hbm = pl.BlockSpec(memory_space=pl.ANY)
    dma = pltpu.SemaphoreType.DMA
    out, dg = pl.pallas_call(
        functools.partial(kernel, n, pipes),
        out_shape=(
            jax.ShapeDtypeStruct((tok, dim), BF16),
            jax.ShapeDtypeStruct((hid, dim), BF16),
        ),
        in_specs=[vmem, vmem, vmem, vmem, smem, vmem, hbm, hbm, hbm, hbm, hbm],
        out_specs=(vmem, hbm),
        scratch_shapes=[
            pltpu.VMEM((4, HALVES, n, CAP, dim // HALVES), BF16),
            pltpu.VMEM((4, HALVES, n, CAP, dim // HALVES), BF16),
            pltpu.VMEM((n, 16, width), BF16),
            pltpu.VMEM((n, 16, width), BF16),
            pltpu.VMEM((2, 16, width), BF16),
            pltpu.VMEM((2, n, 16, width), BF16),
            pltpu.VMEM((HALVES, tok, dim // HALVES), BF16),
            pltpu.VMEM((HALVES, tok, dim // HALVES), BF16),
            pltpu.VMEM((tok, dim), BF16),
            pltpu.VMEM((2, width, dim), BF16),
            pltpu.VMEM((2, width, hid), BF16),
            pltpu.VMEM((2, hid, width), BF16),
            pltpu.VMEM((width, hid), BF16),
            pltpu.VMEM((width, hid), BF16),
            pltpu.VMEM((hid, dim), BF16),
            pltpu.VMEM((2, width, hid), BF16),
            pltpu.VMEM((2, width, hid), BF16),
            pltpu.VMEM((hid, dim), BF16),
            pltpu.VMEM((hid, dim), BF16),
            pltpu.VMEM((hid, dim), BF16),
            dma((4, HALVES, n)), dma((4, HALVES, n)), dma((n,)), dma((n,)), dma((2, n)), dma((2, n)), dma((2, HALVES)), dma((5,)),
        ],
        compiler_params=pltpu.CompilerParams(
            collective_id=0, has_side_effects=True, vmem_limit_bytes=56 * 1024 * 1024
        ),
        cost_estimate=pl.CostEstimate(
            flops=16 * hid * width * dim, bytes_accessed=8 * hid * dim, transcendentals=2 * hid * width
        ),
    )(
        grad_in[0], head_grad, jnp.swapaxes(router_logits[0], 1, 2), jnp.swapaxes(route_ids[0], 1, 2), z_weight.reshape(1, 1),
        router_weight[0].T, jnp.swapaxes(gate_act[0], 1, 2), jnp.swapaxes(up_act[0], 1, 2), gate_weight[0], up_weight[0], down_weight[0],
    )
    return out[None], dg[None]


def solution(mesh):
    return jax.shard_map(
        per_device,
        mesh=mesh,
        in_specs=(
            P("pipe", "expert", None),
            P("expert", None),
            P("pipe", None, "expert", None),
            P("pipe", None, "expert", None),
            P("pipe", None, "expert", None),
            P("pipe", None, "expert", None),
            P("pipe", None, None),
            P("pipe", "expert", None),
            P("pipe", "expert", None),
            P("pipe", "expert", None),
            P(),
        ),
        out_specs=(P("pipe", "expert", None), P("pipe", "expert", None)),
        check_vma=False,
    )
```

```python
import functools

import jax
import jax.numpy as jnp
from jax import lax
from jax.experimental import pallas as pl
from jax.experimental.pallas import tpu as pltpu
from jax.sharding import PartitionSpec as P

EXPERTS = 8
CAP = 24
TOP = 2
F32 = jnp.float32
BF16 = jnp.bfloat16
D0, R0, D1, R1 = 0, 1, 2, 3
HALVES = 2


def iota_f(shape, dim):
    return lax.broadcasted_iota(jnp.int32, shape, dim).astype(F32)


def dot(a, b):
    return jnp.dot(a, b, preferred_element_type=F32)


def kernel(
    n, pipes,
    grad_ref, head_ref, logits_ref, ids_ref, zw_ref, wr_ref, ga_hbm, ua_hbm, wg_hbm, wu_hbm, wd_hbm,
    out_ref, dg_hbm,
    sbuf, rbuf, gsend, grecv, psend, precv, hsend, hrecv, g1_ref,
    x_ref, scaled_ref, st_ref, ggt_ref, ugt_ref, dgv, ga_ref, ua_ref, wg_ref, wu_ref, wd_ref,
    ssem, rsem, gssem, grsem, pssem, prsem, hsem, lsem,
):
    me = lax.axis_index("expert")
    pipe = lax.axis_index("pipe")
    down = lax.rem(pipe + pipes - 1, pipes)
    up = lax.rem(pipe + 1, pipes)
    slices = n // EXPERTS
    tok, dim = grad_ref.shape
    hid = wd_ref.shape[0]
    width = n * CAP
    part = dim // HALVES
    cols = 512 if part % 512 == 0 else part
    ht = 256 if hid % 256 == 0 else hid

    loads = [
        pltpu.make_async_copy(src, dst, lsem.at[i])
        for i, (src, dst) in enumerate(
            [(wd_hbm, wd_ref), (ga_hbm, ga_ref), (ua_hbm, ua_ref), (wg_hbm, wg_ref), (wu_hbm, wu_ref)]
        )
    ]
    for load in loads:
        load.start()

    barrier = pltpu.get_barrier_semaphore()

    def greet(p, carry):
        pl.semaphore_signal(
            barrier, inc=1, device_id=(pipe, lax.rem(me + p, n)), device_id_type=pl.DeviceIdType.MESH
        )
        return carry

    lax.fori_loop(1, n, greet, 0)
    for other in (down, up):
        pl.semaphore_signal(barrier, inc=1, device_id=(other, me), device_id_type=pl.DeviceIdType.MESH)

    def peer_copy(src, dst, s, r, p):
        return pltpu.make_async_remote_copy(
            src_ref=src, dst_ref=dst, send_sem=s, recv_sem=r,
            device_id=(pipe, p), device_id_type=pl.DeviceIdType.MESH,
        )

    def each_peer(body, first_step=1):
        def step(p, carry):
            body(lax.rem(me + 1 + lax.rem(p + first_step + n - 3, n - 1), n))
            return carry

        lax.fori_loop(1, n, step, 0)

    def tiles(total, size, body):
        def step(i, carry):
            body(pl.ds(pl.multiple_of(i * size, size), size))
            return carry

        lax.fori_loop(0, total // size, step, 0)

    def route(m):
        z = logits_ref[m].T
        ids = ids_ref[m].astype(F32)
        ecol = iota_f((tok, EXPERTS), 1)
        picks = [jnp.broadcast_to(ids[k : k + 1], (EXPERTS, tok)).T[:, 0:1] for k in range(TOP)]
        named = [jnp.where(i == ecol, 1.0, 0.0) for i in picks]
        lower = jnp.where(iota_f((tok, tok), 0) > iota_f((tok, tok), 1), 1.0, 0.0).astype(BF16)
        earlier = dot(lower, (named[0] + named[1]).astype(BF16))
        ranks = [jnp.sum(a * earlier, axis=1, keepdims=True) for a in named]
        chosen = [jnp.sum(a * z, axis=1, keepdims=True) for a in named]
        top = jnp.maximum(chosen[0], chosen[1])
        w = [jnp.exp(c - top) for c in chosen]
        gates = [v / (w[0] + w[1]) for v in w]
        q = iota_f((tok, EXPERTS * CAP), 1)
        spread = sum(jnp.where(i * CAP + r == q, 1.0, 0.0) for i, r in zip(picks, ranks))
        if slices == 1:
            gather = spread.astype(BF16)
        else:
            q = iota_f((tok, width), 1)
            member = jnp.floor((q + 0.5) / CAP)
            place = jnp.floor((member + 0.5) / slices) * CAP + (q - member * CAP)
            gather = sum(jnp.where(i * CAP + r == place, 1.0, 0.0) for i, r in zip(picks, ranks)).astype(BF16)
        owner = jnp.floor((iota_f((tok, n), 1) + 0.5) / slices)
        owned = [jnp.where(i == owner, 1.0, 0.0) for i in picks]
        lane = iota_f((tok, width), 1)
        base = (me * CAP).astype(F32)
        at = [jnp.where(r + base == lane, 1.0, 0.0) for r in ranks]
        gate_rows = sum(
            dot((o * g.astype(BF16).astype(F32)).T.astype(BF16), a.astype(BF16))
            for o, g, a in zip(owned, gates, at)
        )
        z_top = jnp.max(z, axis=1, keepdims=True)
        shifted = jnp.exp(z - z_top)
        denom = jnp.sum(shifted, axis=1, keepdims=True)
        z_term = zw_ref[0, 0] * 2.0 * (z_top + jnp.log(denom)) * (shifted / denom)
        return dict(
            named=named, gates=gates, spread_t=spread.T.astype(BF16), gather=gather, owned=owned, at=at,
            gate_rows=gate_rows, z_term=z_term,
        )

    def send_rows(phase, h, by_expert):
        def go(d):
            src = sbuf.at[phase, h, d // slices if by_expert else d]
            peer_copy(src, rbuf.at[phase, h, me], ssem.at[phase, h, d], rsem.at[phase, h, me], d).start()

        each_peer(go, n // 2 - 1)

    def wait_rows(phase, h):
        def go(d):
            ref = rbuf.at[phase, h, d]
            peer_copy(ref, ref, ssem.at[phase, h, d], rsem.at[phase, h, d], d).wait_recv()

        each_peer(go)

    def half_tiles(body):
        for i in range(part // cols):
            body(slice(i * cols, (i + 1) * cols))

    def dispatch(phase, h, spread_t, src):
        def body(c):
            rows = dot(spread_t, src[:, h * part + c.start : h * part + c.stop])
            for e in range(EXPERTS):
                sbuf[phase, h, e, :, c] = rows[e * CAP : (e + 1) * CAP].astype(BF16)

        half_tiles(body)
        send_rows(phase, h, True)
        rbuf[phase, h, me] = sbuf[phase, h, me // slices]

    def joined(phase, h, c):
        return jnp.concatenate([rbuf[phase, h, j, :, c].astype(F32) for j in range(n)], axis=0).astype(BF16)

    def local(m, phase, gate_col):
        for h in range(HALVES):
            wait_rows(phase, h)

            def fill(c):
                x_ref[m, :, h * part + c.start : h * part + c.stop] = joined(phase, h, c)

            half_tiles(fill)
        prob = jnp.zeros((width, 1), F32)
        for h in range(0, hid, ht):
            rows = slice(h, h + ht)
            raw = lax.dot_general(
                x_ref[m], wd_ref[rows, :], (((1,), (1,)), ((), ())), preferred_element_type=F32
            )
            g = ga_ref[m, :, rows].astype(F32)
            u = ua_ref[m, :, rows].astype(F32)
            logistic = jax.nn.sigmoid(g)
            swish = g * logistic
            hidden = swish * u
            prob = prob + jnp.sum(hidden * raw, axis=1, keepdims=True)
            hid_grad = gate_col * raw
            gate_grad = hid_grad * u * logistic * (1.0 + g * (1.0 - logistic))
            scaled_ref[m, :, rows] = (hidden * gate_col).astype(BF16)
            ggt_ref[:, rows] = gate_grad.astype(BF16)
            ugt_ref[:, rows] = (hid_grad * swish).astype(BF16)
        psend[m] = jnp.broadcast_to(prob, (width, 128)).T[0:16].astype(BF16)

    def give_back(m, phase):
        def go(d):
            peer_copy(psend.at[m], precv.at[m, me], pssem.at[m, d], prsem.at[m, me], d).start()

        each_peer(go)
        for h in range(HALVES):

            def body(c):
                w = slice(h * part + c.start, h * part + c.stop)
                total = dot(ggt_ref[...], wg_ref[:, w]) + dot(ugt_ref[...], wu_ref[:, w])
                for j in range(n):
                    sbuf[phase, h, j, :, c] = total[j * CAP : (j + 1) * CAP].astype(BF16)

            half_tiles(body)
            send_rows(phase, h, False)
            rbuf[phase, h, me] = sbuf[phase, h, me]
        precv[m, me] = psend[m]

    def logits_back(m, info):
        def arrived(d):
            peer_copy(psend.at[m], precv.at[m, d], pssem.at[m, d], prsem.at[m, d], d).wait_recv()

        each_peer(arrived)
        probs = [jnp.zeros((tok, width), F32) for _ in range(TOP)]
        for d in range(n):
            row = precv[m, d].astype(F32)[0:1]
            probs = [p + o[:, d : d + 1] * row for p, o in zip(probs, info["owned"])]
        probs = [jnp.sum(p * a, axis=1, keepdims=True) for p, a in zip(probs, info["at"])]
        gates = info["gates"]
        mean = gates[0] * probs[0] + gates[1] * probs[1]
        logit = info["z_term"]
        for k in range(TOP):
            logit = logit + info["named"][k] * (gates[k] * (probs[k] - mean))
        return logit.astype(BF16)

    def combine(phase, h, info, logit, src, store_to):
        wait_rows(phase, h)

        def body(c):
            w = slice(h * part + c.start, h * part + c.stop)
            total = src[:, w].astype(F32) + dot(info["gather"], joined(phase, h, c))
            store_to(h, c, w, (total + dot(logit, wr_ref[:, w])).astype(BF16))

        half_tiles(body)

    first = route(0)
    pl.semaphore_wait(barrier, n + 1)
    for h in range(HALVES):
        dispatch(D0, h, first["spread_t"], grad_ref)
    second = route(1)
    half = lax.broadcasted_iota(jnp.int32, (16, width), 0) < 8
    for d in range(n):
        gsend[d] = jnp.where(half, first["gate_rows"][d : d + 1], second["gate_rows"][d : d + 1]).astype(BF16)

    def go_gates(d):
        peer_copy(gsend.at[d], grecv.at[me], gssem.at[d], grsem.at[me], d).start()

    each_peer(go_gates)
    grecv[me] = gsend[me]

    def come_gates(d):
        peer_copy(gsend.at[d], grecv.at[d], gssem.at[d], grsem.at[d], d).wait_recv()

    each_peer(come_gates)
    gate_all = jnp.zeros((16, width), F32)
    for j in range(n):
        gate_all = gate_all + grecv[j].astype(F32)

    for load in loads:
        load.wait()
    gate_cols = gate_all.T
    local(0, D0, gate_cols[:, 0:1])
    give_back(0, R0)
    logit = logits_back(0, first)

    def keep(h, c, w, value):
        hsend[h, :, c] = value

    def pass_on(h):
        return pltpu.make_async_remote_copy(
            src_ref=hsend.at[h], dst_ref=hrecv.at[h], send_sem=hsem.at[0, h], recv_sem=hsem.at[1, h],
            device_id=(down, me), device_id_type=pl.DeviceIdType.MESH,
        )

    is_last = pipe == pipes - 1
    for h in range(HALVES):
        combine(R0, h, first, logit, grad_ref, keep)
        pass_on(h).start()
    for h in range(HALVES):
        pass_on(h).wait_recv()
        w = slice(h * part, (h + 1) * part)
        g1_ref[:, w] = jnp.where(is_last, head_ref[:, w], hrecv[h])
        dispatch(D1, h, second["spread_t"], g1_ref)
    local(1, D1, gate_cols[:, 8:9])
    give_back(1, R1)

    for m in range(2):
        st_ref[m] = scaled_ref[m].astype(F32).T.astype(BF16)

    def weigh(c):
        total = dot(st_ref[0], x_ref[0, :, c]) + dot(st_ref[1], x_ref[1, :, c])
        dgv[:, c] = total.astype(BF16)

    tiles(dim, 256 if dim % 256 == 0 else dim, weigh)
    store = pltpu.make_async_copy(dgv, dg_hbm, lsem.at[0])
    store.start()
    logit = logits_back(1, second)

    def write(h, c, w, value):
        out_ref[:, w] = value

    for h in range(HALVES):
        combine(R1, h, second, logit, g1_ref, write)
    store.wait()
    for h in range(HALVES):
        pass_on(h).wait_send()

    def drain(d):
        for phase in range(4):
            for h in range(HALVES):
                src = sbuf.at[phase, h, d]
                peer_copy(src, src, ssem.at[phase, h, d], rsem.at[phase, h, d], d).wait_send()
        for m in range(2):
            peer_copy(psend.at[m], precv.at[m, d], pssem.at[m, d], prsem.at[m, d], d).wait_send()
        peer_copy(gsend.at[d], grecv.at[d], gssem.at[d], grsem.at[d], d).wait_send()

    each_peer(drain)


def per_device(
    grad_in, head_grad, router_logits, route_ids, gate_act, up_act, router_weight,
    gate_weight, up_weight, down_weight, z_weight,
):
    n = lax.axis_size("expert")
    pipes = lax.axis_size("pipe")
    tok, dim = head_grad.shape
    hid = down_weight.shape[1]
    width = n * CAP
    vmem = pl.BlockSpec(memory_space=pltpu.VMEM)
    smem = pl.BlockSpec(memory_space=pltpu.SMEM)
    hbm = pl.BlockSpec(memory_space=pl.ANY)
    dma = pltpu.SemaphoreType.DMA
    out, dg = pl.pallas_call(
        functools.partial(kernel, n, pipes),
        out_shape=(
            jax.ShapeDtypeStruct((tok, dim), BF16),
            jax.ShapeDtypeStruct((hid, dim), BF16),
        ),
        in_specs=[vmem, vmem, vmem, vmem, smem, vmem, hbm, hbm, hbm, hbm, hbm],
        out_specs=(vmem, hbm),
        scratch_shapes=[
            pltpu.VMEM((4, HALVES, n, CAP, dim // HALVES), BF16),
            pltpu.VMEM((4, HALVES, n, CAP, dim // HALVES), BF16),
            pltpu.VMEM((n, 16, width), BF16),
            pltpu.VMEM((n, 16, width), BF16),
            pltpu.VMEM((2, 16, width), BF16),
            pltpu.VMEM((2, n, 16, width), BF16),
            pltpu.VMEM((HALVES, tok, dim // HALVES), BF16),
            pltpu.VMEM((HALVES, tok, dim // HALVES), BF16),
            pltpu.VMEM((tok, dim), BF16),
            pltpu.VMEM((2, width, dim), BF16),
            pltpu.VMEM((2, width, hid), BF16),
            pltpu.VMEM((2, hid, width), BF16),
            pltpu.VMEM((width, hid), BF16),
            pltpu.VMEM((width, hid), BF16),
            pltpu.VMEM((hid, dim), BF16),
            pltpu.VMEM((2, width, hid), BF16),
            pltpu.VMEM((2, width, hid), BF16),
            pltpu.VMEM((hid, dim), BF16),
            pltpu.VMEM((hid, dim), BF16),
            pltpu.VMEM((hid, dim), BF16),
            dma((4, HALVES, n)), dma((4, HALVES, n)), dma((n,)), dma((n,)), dma((2, n)), dma((2, n)), dma((2, HALVES)), dma((5,)),
        ],
        compiler_params=pltpu.CompilerParams(
            collective_id=0, has_side_effects=True, vmem_limit_bytes=56 * 1024 * 1024
        ),
        cost_estimate=pl.CostEstimate(
            flops=16 * hid * width * dim, bytes_accessed=8 * hid * dim, transcendentals=2 * hid * width
        ),
    )(
        grad_in[0], head_grad, jnp.swapaxes(router_logits[0], 1, 2), jnp.swapaxes(route_ids[0], 1, 2), z_weight.reshape(1, 1),
        router_weight[0].T, jnp.swapaxes(gate_act[0], 1, 2), jnp.swapaxes(up_act[0], 1, 2), gate_weight[0], up_weight[0], down_weight[0],
    )
    return out[None], dg[None]


def solution(mesh):
    return jax.shard_map(
        per_device,
        mesh=mesh,
        in_specs=(
            P("pipe", "expert", None),
            P("expert", None),
            P("pipe", None, "expert", None),
            P("pipe", None, "expert", None),
            P("pipe", None, "expert", None),
            P("pipe", None, "expert", None),
            P("pipe", None, None),
            P("pipe", "expert", None),
            P("pipe", "expert", None),
            P("pipe", "expert", None),
            P(),
        ),
        out_specs=(P("pipe", "expert", None), P("pipe", "expert", None)),
        check_vma=False,
    )
```

```python
import functools

import jax
import jax.numpy as jnp
from jax import lax
from jax.experimental import pallas as pl
from jax.experimental.pallas import tpu as pltpu
from jax.sharding import PartitionSpec as P

EXPERTS = 8
CAP = 24
TOP = 2
F32 = jnp.float32
BF16 = jnp.bfloat16
D0, R0, D1, R1 = 0, 1, 2, 3
HALVES = 2


def iota_f(shape, dim):
    return lax.broadcasted_iota(jnp.int32, shape, dim).astype(F32)


def dot(a, b):
    return jnp.dot(a, b, preferred_element_type=F32)


def kernel(
    n, pipes,
    grad_ref, head_ref, logits_ref, ids_ref, zw_ref, wr_ref, ga_hbm, ua_hbm, wg_hbm, wu_hbm, wd_hbm,
    out_ref, dg_hbm,
    sbuf, rbuf, gsend, grecv, psend, precv, hsend, hrecv, g1_ref,
    x_ref, scaled_ref, st_ref, ggt_ref, ugt_ref, dgv, ga_ref, ua_ref, wg_ref, wu_ref, wd_ref,
    ssem, rsem, gssem, grsem, pssem, prsem, hsem, lsem,
):
    me = lax.axis_index("expert")
    pipe = lax.axis_index("pipe")
    down = lax.rem(pipe + pipes - 1, pipes)
    up = lax.rem(pipe + 1, pipes)
    slices = n // EXPERTS
    tok, dim = grad_ref.shape
    hid = wd_ref.shape[0]
    width = n * CAP
    part = dim // HALVES
    cols = 512 if part % 512 == 0 else part
    ht = 256 if hid % 256 == 0 else hid

    loads = [
        pltpu.make_async_copy(src, dst, lsem.at[i])
        for i, (src, dst) in enumerate(
            [(wd_hbm, wd_ref), (ga_hbm, ga_ref), (ua_hbm, ua_ref), (wg_hbm, wg_ref), (wu_hbm, wu_ref)]
        )
    ]
    for load in loads:
        load.start()

    barrier = pltpu.get_barrier_semaphore()

    def greet(p, carry):
        pl.semaphore_signal(
            barrier, inc=1, device_id=(pipe, lax.rem(me + p, n)), device_id_type=pl.DeviceIdType.MESH
        )
        return carry

    lax.fori_loop(1, n, greet, 0)
    for other in (down, up):
        pl.semaphore_signal(barrier, inc=1, device_id=(other, me), device_id_type=pl.DeviceIdType.MESH)

    def peer_copy(src, dst, s, r, p):
        return pltpu.make_async_remote_copy(
            src_ref=src, dst_ref=dst, send_sem=s, recv_sem=r,
            device_id=(pipe, p), device_id_type=pl.DeviceIdType.MESH,
        )

    def each_peer(body, first_step=1):
        def step(p, carry):
            body(lax.rem(me + 1 + lax.rem(p + first_step + n - 3, n - 1), n))
            return carry

        lax.fori_loop(1, n, step, 0)

    def tiles(total, size, body):
        def step(i, carry):
            body(pl.ds(pl.multiple_of(i * size, size), size))
            return carry

        lax.fori_loop(0, total // size, step, 0)

    def route(m):
        z = logits_ref[m].T
        ids = ids_ref[m].astype(F32)
        ecol = iota_f((tok, EXPERTS), 1)
        picks = [jnp.broadcast_to(ids[k : k + 1], (EXPERTS, tok)).T[:, 0:1] for k in range(TOP)]
        named = [jnp.where(i == ecol, 1.0, 0.0) for i in picks]
        lower = jnp.where(iota_f((tok, tok), 0) > iota_f((tok, tok), 1), 1.0, 0.0).astype(BF16)
        earlier = dot(lower, (named[0] + named[1]).astype(BF16))
        ranks = [jnp.sum(a * earlier, axis=1, keepdims=True) for a in named]
        chosen = [jnp.sum(a * z, axis=1, keepdims=True) for a in named]
        top = jnp.maximum(chosen[0], chosen[1])
        w = [jnp.exp(c - top) for c in chosen]
        gates = [v / (w[0] + w[1]) for v in w]
        q = iota_f((tok, EXPERTS * CAP), 1)
        spread = sum(jnp.where(i * CAP + r == q, 1.0, 0.0) for i, r in zip(picks, ranks))
        if slices == 1:
            gather = spread.astype(BF16)
        else:
            q = iota_f((tok, width), 1)
            member = jnp.floor((q + 0.5) / CAP)
            place = jnp.floor((member + 0.5) / slices) * CAP + (q - member * CAP)
            gather = sum(jnp.where(i * CAP + r == place, 1.0, 0.0) for i, r in zip(picks, ranks)).astype(BF16)
        owner = jnp.floor((iota_f((tok, n), 1) + 0.5) / slices)
        owned = [jnp.where(i == owner, 1.0, 0.0) for i in picks]
        lane = iota_f((tok, width), 1)
        base = (me * CAP).astype(F32)
        at = [jnp.where(r + base == lane, 1.0, 0.0) for r in ranks]
        gate_rows = sum(
            dot((o * g.astype(BF16).astype(F32)).T.astype(BF16), a.astype(BF16))
            for o, g, a in zip(owned, gates, at)
        )
        z_top = jnp.max(z, axis=1, keepdims=True)
        shifted = jnp.exp(z - z_top)
        denom = jnp.sum(shifted, axis=1, keepdims=True)
        z_term = zw_ref[0, 0] * 2.0 * (z_top + jnp.log(denom)) * (shifted / denom)
        return dict(
            named=named, gates=gates, spread_t=spread.T.astype(BF16), gather=gather, owned=owned, at=at,
            gate_rows=gate_rows, z_term=z_term,
        )

    def send_rows(phase, h, by_expert):
        def go(d):
            src = sbuf.at[phase, h, d // slices if by_expert else d]
            peer_copy(src, rbuf.at[phase, h, me], ssem.at[phase, h, d], rsem.at[phase, h, me], d).start()

        each_peer(go, n // 2 - 1)

    def wait_rows(phase, h):
        def go(d):
            ref = rbuf.at[phase, h, d]
            peer_copy(ref, ref, ssem.at[phase, h, d], rsem.at[phase, h, d], d).wait_recv()

        each_peer(go)

    def half_tiles(body):
        for i in range(part // cols):
            body(slice(i * cols, (i + 1) * cols))

    def dispatch(phase, h, spread_t, src):
        def body(c):
            rows = dot(spread_t, src[:, h * part + c.start : h * part + c.stop])
            for e in range(EXPERTS):
                sbuf[phase, h, e, :, c] = rows[e * CAP : (e + 1) * CAP].astype(BF16)

        half_tiles(body)
        send_rows(phase, h, True)
        rbuf[phase, h, me] = sbuf[phase, h, me // slices]

    def joined(phase, h, c):
        return jnp.concatenate([rbuf[phase, h, j, :, c].astype(F32) for j in range(n)], axis=0).astype(BF16)

    def local(m, phase, gate_col):
        for h in range(HALVES):
            wait_rows(phase, h)

            def fill(c):
                x_ref[m, :, h * part + c.start : h * part + c.stop] = joined(phase, h, c)

            half_tiles(fill)
        prob = jnp.zeros((width, 1), F32)
        for h in range(0, hid, ht):
            rows = slice(h, h + ht)
            raw = lax.dot_general(
                x_ref[m], wd_ref[rows, :], (((1,), (1,)), ((), ())), preferred_element_type=F32
            )
            g = ga_ref[m, :, rows].astype(F32)
            u = ua_ref[m, :, rows].astype(F32)
            logistic = jax.nn.sigmoid(g)
            swish = g * logistic
            hidden = swish * u
            prob = prob + jnp.sum(hidden * raw, axis=1, keepdims=True)
            hid_grad = gate_col * raw
            gate_grad = hid_grad * u * logistic * (1.0 + g * (1.0 - logistic))
            scaled_ref[m, :, rows] = (hidden * gate_col).astype(BF16)
            ggt_ref[:, rows] = gate_grad.astype(BF16)
            ugt_ref[:, rows] = (hid_grad * swish).astype(BF16)
        psend[m] = jnp.broadcast_to(prob, (width, 128)).T[0:16].astype(BF16)

    def give_back(m, phase):
        def go(d):
            peer_copy(psend.at[m], precv.at[m, me], pssem.at[m, d], prsem.at[m, me], d).start()

        each_peer(go)
        for h in range(HALVES):

            def body(c):
                w = slice(h * part + c.start, h * part + c.stop)
                total = dot(ggt_ref[...], wg_ref[:, w]) + dot(ugt_ref[...], wu_ref[:, w])
                for j in range(n):
                    sbuf[phase, h, j, :, c] = total[j * CAP : (j + 1) * CAP].astype(BF16)

            half_tiles(body)
            send_rows(phase, h, False)
            rbuf[phase, h, me] = sbuf[phase, h, me]
        precv[m, me] = psend[m]

    def logits_back(m, info):
        def arrived(d):
            peer_copy(psend.at[m], precv.at[m, d], pssem.at[m, d], prsem.at[m, d], d).wait_recv()

        each_peer(arrived)
        probs = [jnp.zeros((tok, width), F32) for _ in range(TOP)]
        for d in range(n):
            row = precv[m, d].astype(F32)[0:1]
            probs = [p + o[:, d : d + 1] * row for p, o in zip(probs, info["owned"])]
        probs = [jnp.sum(p * a, axis=1, keepdims=True) for p, a in zip(probs, info["at"])]
        gates = info["gates"]
        mean = gates[0] * probs[0] + gates[1] * probs[1]
        logit = info["z_term"]
        for k in range(TOP):
            logit = logit + info["named"][k] * (gates[k] * (probs[k] - mean))
        return logit.astype(BF16)

    def combine(phase, h, info, logit, src, store_to):
        wait_rows(phase, h)

        def body(c):
            w = slice(h * part + c.start, h * part + c.stop)
            total = src[:, w].astype(F32) + dot(info["gather"], joined(phase, h, c))
            store_to(h, c, w, (total + dot(logit, wr_ref[:, w])).astype(BF16))

        half_tiles(body)

    first = route(0)
    pl.semaphore_wait(barrier, n + 1)
    for h in range(HALVES):
        dispatch(D0, h, first["spread_t"], grad_ref)
    second = route(1)
    half = lax.broadcasted_iota(jnp.int32, (16, width), 0) < 8
    for d in range(n):
        gsend[d] = jnp.where(half, first["gate_rows"][d : d + 1], second["gate_rows"][d : d + 1]).astype(BF16)

    def go_gates(d):
        peer_copy(gsend.at[d], grecv.at[me], gssem.at[d], grsem.at[me], d).start()

    each_peer(go_gates)
    grecv[me] = gsend[me]

    def come_gates(d):
        peer_copy(gsend.at[d], grecv.at[d], gssem.at[d], grsem.at[d], d).wait_recv()

    each_peer(come_gates)
    gate_all = jnp.zeros((16, width), F32)
    for j in range(n):
        gate_all = gate_all + grecv[j].astype(F32)

    for load in loads:
        load.wait()
    gate_cols = gate_all.T
    local(0, D0, gate_cols[:, 0:1])
    give_back(0, R0)
    logit = logits_back(0, first)

    def keep(h, c, w, value):
        hsend[h, :, c] = value

    def pass_on(h):
        return pltpu.make_async_remote_copy(
            src_ref=hsend.at[h], dst_ref=hrecv.at[h], send_sem=hsem.at[0, h], recv_sem=hsem.at[1, h],
            device_id=(down, me), device_id_type=pl.DeviceIdType.MESH,
        )

    is_last = pipe == pipes - 1
    for h in range(HALVES):
        combine(R0, h, first, logit, grad_ref, keep)
        pass_on(h).start()
    for h in range(HALVES):
        pass_on(h).wait_recv()
        w = slice(h * part, (h + 1) * part)
        g1_ref[:, w] = jnp.where(is_last, head_ref[:, w], hrecv[h])
        dispatch(D1, h, second["spread_t"], g1_ref)
    local(1, D1, gate_cols[:, 8:9])
    give_back(1, R1)

    for m in range(2):
        st_ref[m] = scaled_ref[m].astype(F32).T.astype(BF16)

    def weigh(c):
        total = dot(st_ref[0], x_ref[0, :, c]) + dot(st_ref[1], x_ref[1, :, c])
        dgv[:, c] = total.astype(BF16)

    tiles(dim, 256 if dim % 256 == 0 else dim, weigh)
    store = pltpu.make_async_copy(dgv, dg_hbm, lsem.at[0])
    store.start()
    logit = logits_back(1, second)

    def write(h, c, w, value):
        out_ref[:, w] = value

    for h in range(HALVES):
        combine(R1, h, second, logit, g1_ref, write)
    store.wait()
    for h in range(HALVES):
        pass_on(h).wait_send()

    def drain(d):
        for phase in range(4):
            for h in range(HALVES):
                src = sbuf.at[phase, h, d]
                peer_copy(src, src, ssem.at[phase, h, d], rsem.at[phase, h, d], d).wait_send()
        for m in range(2):
            peer_copy(psend.at[m], precv.at[m, d], pssem.at[m, d], prsem.at[m, d], d).wait_send()
        peer_copy(gsend.at[d], grecv.at[d], gssem.at[d], grsem.at[d], d).wait_send()

    each_peer(drain)


def hand_on(pieces, out_src, dg_src, out_dst, dg_dst, sems):
    rows = dg_src.shape[0] // pieces
    if rows % 16:
        pieces, rows = 1, dg_src.shape[0]
    copies = [
        pltpu.make_async_copy(
            dg_src.at[pl.ds(i * rows, rows)], dg_dst.at[pl.ds(i * rows, rows)], sems.at[i]
        )
        for i in range(pieces)
    ]
    copies.append(pltpu.make_async_copy(out_src, out_dst, sems.at[pieces]))
    for copy in copies:
        copy.start()
    for copy in copies:
        copy.wait()


def per_device(
    grad_in, head_grad, router_logits, route_ids, gate_act, up_act, router_weight,
    gate_weight, up_weight, down_weight, z_weight,
):
    n = lax.axis_size("expert")
    pipes = lax.axis_size("pipe")
    tok, dim = head_grad.shape
    hid = down_weight.shape[1]
    width = n * CAP
    vmem = pl.BlockSpec(memory_space=pltpu.VMEM)
    smem = pl.BlockSpec(memory_space=pltpu.SMEM)
    hbm = pl.BlockSpec(memory_space=pl.ANY)
    dma = pltpu.SemaphoreType.DMA
    out, dg = pl.pallas_call(
        functools.partial(kernel, n, pipes),
        out_shape=(
            jax.ShapeDtypeStruct((tok, dim), BF16),
            jax.ShapeDtypeStruct((hid, dim), BF16),
        ),
        in_specs=[vmem, vmem, vmem, vmem, smem, vmem, hbm, hbm, hbm, hbm, hbm],
        out_specs=(vmem, hbm),
        scratch_shapes=[
            pltpu.VMEM((4, HALVES, n, CAP, dim // HALVES), BF16),
            pltpu.VMEM((4, HALVES, n, CAP, dim // HALVES), BF16),
            pltpu.VMEM((n, 16, width), BF16),
            pltpu.VMEM((n, 16, width), BF16),
            pltpu.VMEM((2, 16, width), BF16),
            pltpu.VMEM((2, n, 16, width), BF16),
            pltpu.VMEM((HALVES, tok, dim // HALVES), BF16),
            pltpu.VMEM((HALVES, tok, dim // HALVES), BF16),
            pltpu.VMEM((tok, dim), BF16),
            pltpu.VMEM((2, width, dim), BF16),
            pltpu.VMEM((2, width, hid), BF16),
            pltpu.VMEM((2, hid, width), BF16),
            pltpu.VMEM((width, hid), BF16),
            pltpu.VMEM((width, hid), BF16),
            pltpu.VMEM((hid, dim), BF16),
            pltpu.VMEM((2, width, hid), BF16),
            pltpu.VMEM((2, width, hid), BF16),
            pltpu.VMEM((hid, dim), BF16),
            pltpu.VMEM((hid, dim), BF16),
            pltpu.VMEM((hid, dim), BF16),
            dma((4, HALVES, n)), dma((4, HALVES, n)), dma((n,)), dma((n,)), dma((2, n)), dma((2, n)), dma((2, HALVES)), dma((5,)),
        ],
        compiler_params=pltpu.CompilerParams(
            collective_id=0, has_side_effects=True, vmem_limit_bytes=56 * 1024 * 1024
        ),
        cost_estimate=pl.CostEstimate(
            flops=16 * hid * width * dim, bytes_accessed=8 * hid * dim, transcendentals=2 * hid * width
        ),
    )(
        grad_in[0], head_grad, jnp.swapaxes(router_logits[0], 1, 2), jnp.swapaxes(route_ids[0], 1, 2), z_weight.reshape(1, 1),
        router_weight[0].T, jnp.swapaxes(gate_act[0], 1, 2), jnp.swapaxes(up_act[0], 1, 2), gate_weight[0], up_weight[0], down_weight[0],
    )
    pieces = 8
    out, dg = pl.pallas_call(
        functools.partial(hand_on, pieces),
        out_shape=(
            jax.ShapeDtypeStruct((tok, dim), BF16),
            jax.ShapeDtypeStruct((hid, dim), BF16),
        ),
        in_specs=[hbm, hbm],
        out_specs=(hbm, hbm),
        scratch_shapes=[dma((pieces + 1,))],
        cost_estimate=pl.CostEstimate(flops=0, bytes_accessed=4 * hid * dim, transcendentals=0),
    )(out, dg)
    return out[None], dg[None]


def solution(mesh):
    return jax.shard_map(
        per_device,
        mesh=mesh,
        in_specs=(
            P("pipe", "expert", None),
            P("expert", None),
            P("pipe", None, "expert", None),
            P("pipe", None, "expert", None),
            P("pipe", None, "expert", None),
            P("pipe", None, "expert", None),
            P("pipe", None, None),
            P("pipe", "expert", None),
            P("pipe", "expert", None),
            P("pipe", "expert", None),
            P(),
        ),
        out_specs=(P("pipe", "expert", None), P("pipe", "expert", None)),
        check_vma=False,
    )
```
